32 devices in a mesh: groups: 2 (over y), inst: 16 (over z, x, core).
Axes of the slice: x: 2, y: 2, z: 4, core: 2. Of those that a mesh axis runs over, the one named last changes fastest.
Arguments:
- queries: bfloat16 [8192, 4096], P(('groups', 'inst')), parts along dimension 0, may hold values from -190 to 190
- prefix_kv: bfloat16 [65536, 1024], P(('groups', 'inst')), parts along dimension 0, may hold values from -7 to 7
- span_kv: bfloat16 [8192, 1024], P(('groups', 'inst')), parts along dimension 0, may hold values from -6 to 6
- prefix_blocks: int32 [32], P('groups'), parts along dimension 0, may hold values from 1 to 16, 128 in all
- swap_flags: int32 [32], P('groups'), parts along dimension 0, may hold values from 0 to 1, as said below
- owners: int32 [32, 16], P(('groups', 'inst')), parts along dimension 0, may hold values from 0 to 15, as said below
Outputs:
- attended: bfloat16 [8192, 4096], P(('groups', 'inst')), parts along dimension 0
- decode_pages: bfloat16 [8192, 1024], P(('groups', 'inst')), parts along dimension 0
The draws below stay inside these ranges and needn't reach their ends.
There are 2 independent parts, one for each index of `groups`. The reference program is written for one: setup_inputs(seed, part) draws one part's arguments, and reference() takes and returns one part's arrays. A program takes and returns all parts, laid end to end along the dimension named above; each array names one. Nothing has to cross between parts.
Inputs may be any that keep to these rules, and one draw needn't show every extreme that they name: swap_flags[i] equals swap_flags[(i + 8) mod 16]: paired instances trade their spans together. owners[h, s] = (h + offset[s]) mod 16 with 16 distinct offsets common to all requests: every instance owns exactly one page of each page index.
All inputs are finite; a program needn't handle non-finite values.
Results may differ from the reference program's by a relative error of at most 0.005.
Values may be sent and summed in bfloat16 or wider, within the bound.
No kernel may reach another device: no remote copies, remote signals or barrier semaphores. Data moves between devices by JAX's collectives and lax.ppermute only.
A program may use at most 128 MiB of HBM per device.

```python
import math
import jax
import jax.numpy as jnp
import numpy as np
from jax import lax

HQ = 32
KVH = 4
HD = 128
BLK = 128
CT = 256
PMAX = 2048
INSTANCES = 16
PB = 16
PAGE = 16
NPAGES = 16


def prefix_keys(base_key):
    return jnp.clip(jax.random.normal(base_key, (INSTANCES * PMAX, KVH * HD), jnp.float32), -6.0, 6.0)


def draw_prefix_kv(key, part):
    shared_keys = prefix_keys(key)
    key = jax.random.fold_in(key, 5)
    values = jnp.clip(jax.random.normal(key, (INSTANCES * PMAX, KVH * HD), jnp.float32), -6.0, 6.0)
    return jnp.concatenate([shared_keys, values], axis=1).astype(jnp.bfloat16)


def draw_queries(key, part):
    key = jax.random.fold_in(key, 7)
    query_rows = jnp.clip(jax.random.normal(key, (INSTANCES * CT, HQ * HD), jnp.float32), -6.0, 6.0)
    return query_rows.astype(jnp.bfloat16)


def draw_swap_flags(key, part):
    key = jax.random.fold_in(key, 9)
    lower_flags = jax.random.randint(key, (INSTANCES // 2,), 0, 2)
    lower_flags = lower_flags.at[0].set(1).at[1].set(0)
    return jnp.concatenate([lower_flags, lower_flags]).astype(jnp.int32)


def draw_owners(key, part):
    key = jax.random.fold_in(key, 11)
    offsets = jax.random.permutation(key, INSTANCES)[:NPAGES].astype(jnp.int32)
    requests = jnp.arange(INSTANCES, dtype=jnp.int32)[:, None]
    return ((requests + offsets[None, :]) % INSTANCES).astype(jnp.int32)


def block_scale(stream_key, shape, shards, least, largest):
    gain = 1.0
    for position, blocks in shards:
        heights = jax.random.uniform(jax.random.fold_in(jax.random.fold_in(stream_key, 6), position), (blocks,), jnp.float32, least / len(shards), largest / len(shards))
        gain = gain * jnp.repeat(jnp.exp(heights), shape[position] // blocks).reshape((-1,) + (1,) * (len(shape) - 1 - position))
    return gain


def profile(amount, total, limit, lean):
    loads = [(1 << 20) // math.isqrt(standing ** lean) + 1 for standing in range(2, amount + 1)]
    rest, given = total - limit - (amount - 1), [1] * (amount - 1)
    while rest > 0:
        movable = [i for i in range(amount - 1) if given[i] < limit]
        pool, budget = sum([loads[i] for i in movable]), rest
        for i in movable:
            extra = min(limit - given[i], max(1, budget * loads[i] // pool), rest)
            given[i] = given[i] + extra
            rest = rest - extra
    return np.array([limit] + given)


def uneven_parts(own_key, amount, total, limit, lean):
    if amount == 2:
        one = jax.random.randint(own_key, (), max(1, total - limit), min(limit, total - 1) + 1)
        return jnp.stack([one, total - one])
    tallies = jnp.asarray(profile(amount, total, limit, lean), jnp.int32)
    twos = (amount - 1) // 2
    source_of, taker = tallies[1:1 + 2 * twos:2], tallies[2:2 + 2 * twos:2]
    room = jnp.minimum(source_of - 1, limit - taker)
    passed = jax.random.randint(jax.random.fold_in(own_key, 1), (twos,), 0, 1 << 20) % (room + 1)
    tallies = tallies.at[1:1 + 2 * twos:2].set(source_of - passed).at[2:2 + 2 * twos:2].set(taker + passed)
    return tallies[jax.random.permutation(jax.random.fold_in(own_key, 2), amount)]


def noise(rng, shape, scale, limit, cuts=(), kind=jnp.bfloat16):
    entries = scale * jax.random.normal(rng, shape, jnp.float32)
    if cuts:
        entries = entries * block_scale(rng, shape, cuts, -0.22, 0.18)
    return jnp.clip(entries, -limit, limit).astype(kind)


def setup_inputs(seed: int = 0, part: int = 0) -> dict:
    key_of = jax.random.split(jax.random.key(seed), 7)
    part_keys = jax.random.split(jax.random.fold_in(key_of[6], part), 7)
    queries = draw_queries(jax.random.fold_in(jax.random.fold_in(key_of[6], part), 71), part)
    prefix_kv = draw_prefix_kv(jax.random.fold_in(jax.random.fold_in(key_of[6], part), 71), part)
    span_kv = noise(part_keys[2], (INSTANCES * CT, 2 * KVH * HD), 1.0, 6.0, ((0, 16),))
    prefix_blocks = uneven_parts(part_keys[3], INSTANCES, INSTANCES * PB // 2, PB, 2).astype(jnp.int32)
    swap_flags = draw_swap_flags(jax.random.fold_in(jax.random.fold_in(key_of[6], part), 71), part)
    owners = draw_owners(jax.random.fold_in(jax.random.fold_in(key_of[6], part), 71), part)
    return dict(queries=queries, prefix_kv=prefix_kv, span_kv=span_kv, prefix_blocks=prefix_blocks, swap_flags=swap_flags, owners=owners)


def span_attention(query_rows, prefix_rows, span_rows, prefix_count):
    groups_per = HQ // KVH
    width_kv = KVH * HD
    query_heads = query_rows.astype(jnp.float32).reshape(CT, KVH, groups_per, HD)
    every_kv = jnp.concatenate([prefix_rows, span_rows], axis=0).astype(jnp.float32)
    key_heads = every_kv[:, :width_kv].reshape(PMAX + CT, KVH, HD)
    value_heads = every_kv[:, width_kv:].reshape(PMAX + CT, KVH, HD)
    scores = jnp.einsum('tgah,kgh->gatk', query_heads, key_heads) / math.sqrt(HD)
    key_pos = jnp.arange(PMAX + CT, dtype=jnp.int32)[None, :]
    query_pos = jnp.arange(CT, dtype=jnp.int32)[:, None]
    live_mask = jnp.where(key_pos < PMAX, key_pos < prefix_count * BLK, key_pos - PMAX <= query_pos)
    scores = jnp.where(live_mask, scores, -1e+30)
    row_top = lax.optimization_barrier(jnp.max(scores, axis=-1, keepdims=True))
    weights = jnp.exp(scores - row_top)
    totals = lax.optimization_barrier(jnp.sum(weights, axis=-1, keepdims=True))
    rounded = lax.optimization_barrier(weights.astype(jnp.bfloat16)).astype(jnp.float32)
    mixture = jnp.einsum('gatk,kgh->gath', rounded, value_heads) / totals
    return mixture.transpose(2, 0, 1, 3).reshape(CT, HQ * HD).astype(jnp.bfloat16)

def reference(queries, prefix_kv, span_kv, prefix_blocks, swap_flags, owners):
    width_pair = 2 * KVH * HD
    query_all = queries.reshape(INSTANCES, CT, HQ * HD)
    prefix_all = prefix_kv.reshape(INSTANCES, PMAX, width_pair)
    span_all = span_kv.reshape(INSTANCES, CT, width_pair)
    results = lax.map(lambda packed: span_attention(*packed), (query_all, prefix_all, span_all, prefix_blocks))
    indices = jnp.arange(INSTANCES, dtype=jnp.int32)
    source = jnp.where(swap_flags == 1, (indices + INSTANCES // 2) % INSTANCES, indices)
    attended = results[source].reshape(INSTANCES * CT, HQ * HD)
    offsets = owners[0].astype(jnp.int32)
    senders = ((indices[:, None] - offsets[None, :]) % INSTANCES).astype(jnp.int32)
    page_index = jnp.arange(NPAGES, dtype=jnp.int32)[None, :]
    pages = span_all.reshape(INSTANCES, NPAGES, PAGE, width_pair)
    ordered = pages[senders, page_index]
    decode_pages = ordered.reshape(INSTANCES * CT, width_pair)
    return (attended, decode_pages)
```

```python
import functools
import math

import jax
import jax.numpy as jnp
from jax import lax
from jax.experimental import pallas as pl
from jax.experimental.pallas import tpu as pltpu
from jax.sharding import PartitionSpec as P

HQ = 32
KVH = 4
HD = 128
BLK = 128
GROUP = HQ // KVH

key_rows = 512
lowest = -1e30
to_log2 = math.log2(math.e) / math.sqrt(HD)


def attend_kernel(count_ref, q_ref, k_ref, v_ref, span_k_ref, span_v_ref, out_ref, top_ref, total_ref, acc_ref):
    rows = q_ref.shape[0]
    stacked = rows * GROUP
    queries = jnp.concatenate([q_ref[:, h * HD : (h + 1) * HD] for h in range(GROUP)], 0)

    def tile(keys, values, live, first):
        scores = lax.dot_general(
            queries, keys, (((1,), (1,)), ((), ())), preferred_element_type=jnp.float32
        )
        parts = [scores[:, c * HD : (c + 1) * HD] for c in range(keys.shape[0] // HD)]
        if live is not None:
            parts = [jnp.where(mask, part, lowest) for mask, part in zip(live, parts)]
        top = jnp.max(functools.reduce(jnp.maximum, parts), axis=1, keepdims=True)
        if first:
            top = jnp.broadcast_to(top, (stacked, HD))
        else:
            old = top_ref[...]
            top = jnp.maximum(old, top)
            shrink = jnp.exp2((old - top) * to_log2)
        weights = [jnp.exp2((part - top) * to_log2) for part in parts]
        sums = functools.reduce(jnp.add, weights)
        rounded = jnp.concatenate([w.astype(jnp.bfloat16) for w in weights], 1)
        product = jnp.dot(rounded, values, preferred_element_type=jnp.float32)
        top_ref[...] = top
        if first:
            total_ref[...] = sums
            acc_ref[...] = product
        else:
            total_ref[...] = total_ref[...] * shrink + sums
            acc_ref[...] = acc_ref[...] * shrink + product

    row = lax.broadcasted_iota(jnp.int32, (rows, HD), 0)
    column = lax.broadcasted_iota(jnp.int32, (rows, HD), 1)
    causal = [
        jnp.concatenate([column + c * HD <= row] * GROUP, 0) for c in range(rows // HD)
    ]
    tile(span_k_ref[...], span_v_ref[...], causal, True)

    count = count_ref[0]
    unit = key_rows // BLK
    full = count // unit

    def step(index, carried):
        place = pl.ds(pl.multiple_of(index * key_rows, key_rows), key_rows)
        tile(k_ref[place, :], v_ref[place, :], None, False)
        return carried

    lax.fori_loop(0, full, step, 0)
    for rest in range(1, unit):

        @pl.when(count - full * unit == rest)
        def _():
            place = pl.ds(pl.multiple_of(full * key_rows, key_rows), rest * BLK)
            tile(k_ref[place, :], v_ref[place, :], None, False)

    mixture = acc_ref[...] / jnp.sum(total_ref[...], axis=1, keepdims=True)
    for h in range(GROUP):
        out_ref[:, h * HD : (h + 1) * HD] = mixture[h * rows : (h + 1) * rows].astype(jnp.bfloat16)


def attend(count, queries, prefix_kv, span_kv, first, heads):
    rows = queries.shape[0]
    prefix_rows = prefix_kv.shape[0]
    width = GROUP * HD
    keys = rows + prefix_rows
    state = pltpu.VMEM((rows * GROUP, HD), jnp.float32)
    return pl.pallas_call(
        attend_kernel,
        grid_spec=pltpu.PrefetchScalarGridSpec(
            num_scalar_prefetch=1,
            grid=(heads,),
            in_specs=[
                pl.BlockSpec((rows, width), lambda i, count: (0, first + i)),
                pl.BlockSpec((prefix_rows, HD), lambda i, count: (0, first + i)),
                pl.BlockSpec((prefix_rows, HD), lambda i, count: (0, KVH + first + i)),
                pl.BlockSpec((rows, HD), lambda i, count: (0, first + i)),
                pl.BlockSpec((rows, HD), lambda i, count: (0, KVH + first + i)),
            ],
            out_specs=pl.BlockSpec((rows, width), lambda i, count: (0, i)),
            scratch_shapes=[state, state, state],
        ),
        out_shape=jax.ShapeDtypeStruct((rows, heads * width), jnp.bfloat16),
        compiler_params=pltpu.CompilerParams(vmem_limit_bytes=48 << 20),
        cost_estimate=pl.CostEstimate(
            flops=4 * rows * width * heads * keys // 2,
            bytes_accessed=2 * heads * (2 * rows * width + 2 * keys * HD),
            transcendentals=rows * GROUP * heads * keys // 2,
        ),
        name="attend",
    )(count, queries, prefix_kv, prefix_kv, span_kv, span_kv)


def per_device(queries, prefix_kv, span_kv, prefix_blocks, swap_flags, owners):
    inst_count = lax.axis_size("inst")
    half_count = inst_count // 2
    here = lax.axis_index("inst")
    trade = [(source, (source + half_count) % inst_count) for source in range(inst_count)]
    moved = swap_flags[here] == 1
    count = prefix_blocks[here][None]

    def traded(count, queries, prefix_kv, span_kv):
        parts = [attend(count, queries, prefix_kv, span_kv, g, 1) for g in range(KVH)]
        return jnp.concatenate([lax.ppermute(part, "inst", trade) for part in parts], 1)

    def stayed(count, queries, prefix_kv, span_kv):
        return attend(count, queries, prefix_kv, span_kv, 0, KVH)

    width_pair = span_kv.shape[1]
    page_count = owners.shape[1]
    page_rows = span_kv.shape[0] // page_count
    owner_row = owners[0]
    span_pages = span_kv.reshape(page_count, page_rows, width_pair)
    outgoing = (
        jnp.zeros((inst_count, page_rows, width_pair), span_kv.dtype).at[owner_row].set(span_pages)
    )
    received = lax.all_to_all(outgoing, "inst", split_axis=0, concat_axis=0, tiled=True)
    offsets = (owner_row - here) % inst_count
    senders = (here - offsets) % inst_count
    decode_pages = received[senders].reshape(span_kv.shape[0], width_pair)

    attended = lax.cond(moved, traded, stayed, count, queries, prefix_kv, span_kv)
    return (attended, decode_pages)


def solution(mesh):
    placed = (
        P(("groups", "inst"), None),
        P(("groups", "inst"), None),
        P(("groups", "inst"), None),
        P("groups"),
        P("groups"),
        P(("groups", "inst"), None),
    )
    return jax.shard_map(
        per_device,
        mesh=mesh,
        in_specs=placed,
        out_specs=(P(("groups", "inst"), None), P(("groups", "inst"), None)),
        check_vma=False,
    )
```

```python
import functools
import math

import jax
import jax.numpy as jnp
from jax import lax
from jax.experimental import pallas as pl
from jax.experimental.pallas import tpu as pltpu
from jax.sharding import PartitionSpec as P

HQ = 32
KVH = 4
HD = 128
BLK = 128
GROUP = HQ // KVH

key_rows = 512
lowest = -1e30
to_log2 = math.log2(math.e) / math.sqrt(HD)


def attend_kernel(count_ref, q_ref, k_ref, v_ref, span_k_ref, span_v_ref, out_ref, query_ref, top_ref, total_ref, acc_ref):
    rows = q_ref.shape[0]
    heads = q_ref.shape[1] // HD
    for h in range(heads):
        query_ref[h * rows : (h + 1) * rows, :] = q_ref[:, h * HD : (h + 1) * HD]

    def tile(keys, values, live, dead):
        scores = lax.dot_general(
            query_ref[...], keys, (((1,), (1,)), ((), ())), preferred_element_type=jnp.float32
        )
        parts = [scores[:, c * HD : (c + 1) * HD] for c in range(keys.shape[0] // HD)]
        if live is not None:
            parts = [jnp.where(mask, part, lowest) for mask, part in zip(live, parts)]
        top = jnp.max(functools.reduce(jnp.maximum, parts), axis=1, keepdims=True)
        if dead is None:
            top = jnp.broadcast_to(top, acc_ref.shape)
        else:
            old = top_ref[...]
            top = jnp.maximum(old, top)
            shrink = jnp.exp2((old - top) * to_log2)
        weights = [jnp.exp2((part - top) * to_log2) for part in parts]
        sums = functools.reduce(jnp.add, weights)
        rounded = jnp.concatenate([w.astype(jnp.bfloat16) for w in weights], 1)
        product = jnp.dot(rounded, values, preferred_element_type=jnp.float32)
        top_ref[...] = top
        if dead is None:
            total_ref[...] = sums
            acc_ref[...] = product
        else:
            total_ref[...] = total_ref[...] * shrink + (sums - weights[0] * dead)
            acc_ref[...] = acc_ref[...] * shrink + product

    row = lax.broadcasted_iota(jnp.int32, (rows, HD), 0)
    column = lax.broadcasted_iota(jnp.int32, (rows, HD), 1)
    causal = [
        jnp.concatenate([column + c * HD <= row] * heads, 0) for c in range(rows // HD)
    ]
    tile(span_k_ref[...], span_v_ref[...], causal, None)

    valid = count_ref[lax.axis_index("inst")] * BLK
    position = lax.broadcasted_iota(jnp.int32, (key_rows, HD), 0)
    first_lane = lax.broadcasted_iota(jnp.int32, (1, HD), 1) == 0

    def step(index, carried):
        offset = pl.multiple_of(index * key_rows, key_rows)
        keys = k_ref[pl.ds(offset, key_rows), :]
        values = v_ref[pl.ds(offset, key_rows), :]
        live = position < valid - offset
        keys = jnp.where(live, keys, jnp.broadcast_to(keys[0:1, :], keys.shape))
        values = jnp.where(live, values, jnp.zeros_like(values))
        dead = jnp.maximum(key_rows - (valid - offset), 0).astype(jnp.float32)
        tile(keys, values, None, jnp.where(first_lane, dead, 0.0))
        return carried

    lax.fori_loop(0, (valid + key_rows - 1) // key_rows, step, 0)
    mixture = acc_ref[...] / jnp.sum(total_ref[...], axis=1, keepdims=True)
    for h in range(heads):
        out_ref[:, h * HD : (h + 1) * HD] = mixture[h * rows : (h + 1) * rows].astype(jnp.bfloat16)


def attend(counts, queries, prefix_kv, span_kv, first, heads, per_step):
    rows = queries.shape[0]
    prefix_rows = prefix_kv.shape[0]
    width = per_step * HD
    start = first // per_step
    share = GROUP // per_step
    keys = rows + prefix_rows
    state = pltpu.VMEM((rows * per_step, HD), jnp.float32)
    return pl.pallas_call(
        attend_kernel,
        grid_spec=pltpu.PrefetchScalarGridSpec(
            num_scalar_prefetch=1,
            grid=(heads // per_step,),
            in_specs=[
                pl.BlockSpec((rows, width), lambda i, counts: (0, start + i)),
                pl.BlockSpec((prefix_rows, HD), lambda i, counts: (0, (start + i) // share)),
                pl.BlockSpec((prefix_rows, HD), lambda i, counts: (0, KVH + (start + i) // share)),
                pl.BlockSpec((rows, HD), lambda i, counts: (0, (start + i) // share)),
                pl.BlockSpec((rows, HD), lambda i, counts: (0, KVH + (start + i) // share)),
            ],
            out_specs=pl.BlockSpec((rows, width), lambda i, counts: (0, i)),
            scratch_shapes=[
                pltpu.VMEM((rows * per_step, HD), jnp.bfloat16),
                state,
                state,
                state,
            ],
        ),
        out_shape=jax.ShapeDtypeStruct((rows, heads * HD), jnp.bfloat16),
        compiler_params=pltpu.CompilerParams(vmem_limit_bytes=48 << 20),
        cost_estimate=pl.CostEstimate(
            flops=4 * rows * heads * HD * keys // 2,
            bytes_accessed=2 * (2 * rows * heads * HD + 2 * keys * HD * heads // per_step),
            transcendentals=rows * heads * keys // 2,
        ),
        name="attend",
    )(counts, queries, prefix_kv, prefix_kv, span_kv, span_kv)


def scatter_kernel(owner_ref, span_ref, out_ref, sems):
    rows = out_ref.shape[1]
    copies = []
    for s in range(owner_ref.shape[1]):
        page = span_ref.at[s * rows : (s + 1) * rows, :]
        copies.append(pltpu.make_async_copy(page, out_ref.at[owner_ref[0, s]], sems.at[s]))
    for copy in copies:
        copy.start()
    for copy in copies:
        copy.wait()


def scatter_pages(owners, span_kv, places):
    page_count = owners.shape[1]
    page_rows = span_kv.shape[0] // page_count
    width = span_kv.shape[1]
    return pl.pallas_call(
        scatter_kernel,
        grid_spec=pltpu.PrefetchScalarGridSpec(
            num_scalar_prefetch=1,
            grid=(),
            in_specs=[pl.BlockSpec(memory_space=pltpu.VMEM)],
            out_specs=pl.BlockSpec(memory_space=pl.ANY),
            scratch_shapes=[pltpu.SemaphoreType.DMA((page_count,))],
        ),
        out_shape=jax.ShapeDtypeStruct((places, page_rows, width), span_kv.dtype),
        name="scatter_pages",
    )(owners, span_kv)


part_plan = ((4, False), (8, True), (4, True), (8, False), (8, False))
per_step = 4


def per_device(queries, prefix_kv, span_kv, prefix_blocks, swap_flags, owners):
    inst_count = lax.axis_size("inst")
    half_count = inst_count // 2
    here = lax.axis_index("inst")

    places = jnp.arange(inst_count)
    side = (here >> 1) & 1
    lower = here - 2 * side
    mask = jnp.sum(swap_flags * ((places == lower) * 1 + (places == lower + 2) * 2))
    bases = [i for i in range(inst_count) if not i & 2]

    def far(inst):
        return (inst + half_count) % inst_count

    def send(value, hops):
        return lax.ppermute(value, "inst", hops)

    def branch(flagged):
        def run(side, counts, queries, prefix_kv, span_kv):
            if not flagged:
                return attend(counts, queries, prefix_kv, span_kv, 0, HQ, per_step)
            straight = [(i + 2 * c, far(i) + 2 * c) for c in flagged for i in bases]
            first, came, parts, pending = 0, [], [], []
            for turn, (heads, relay) in enumerate(part_plan):
                if turn == 4 and pending:
                    held, counts = lax.optimization_barrier(([came[at] for at in pending], counts))
                    for at, value in zip(pending, held):
                        came[at] = send(value, over)
                part = attend(counts, queries, prefix_kv, span_kv, first, heads, per_step)
                if relay and len(flagged) == 1:
                    c = flagged[0]
                    over = [(i + 2 * (1 - c), far(i) + 2 * c) for i in bases]
                    came.append(send(part, [(i + 2 * c, i + 2 * (1 - c)) for i in bases]))
                    pending.append(turn)
                else:
                    came.append(send(part, straight))
                parts.append(part)
                first += heads
            if len(flagged) == 1:
                mine = side == flagged[0]
                came = [jnp.where(mine, new, own) for new, own in zip(came, parts)]
            return jnp.concatenate(came, 1)

        return run

    outgoing = scatter_pages(owners, span_kv, inst_count)
    received = lax.all_to_all(outgoing, "inst", split_axis=0, concat_axis=0, tiled=True)
    branches = [branch([c for c in (0, 1) if m >> c & 1]) for m in range(4)]
    attended = lax.switch(mask, branches, side, prefix_blocks, queries, prefix_kv, span_kv)
    offsets = (owners[0] - here) % inst_count
    senders = (here - offsets) % inst_count
    decode_pages = received[senders].reshape(span_kv.shape)
    return (attended, decode_pages)


def solution(mesh):
    placed = (
        P(("groups", "inst"), None),
        P(("groups", "inst"), None),
        P(("groups", "inst"), None),
        P("groups"),
        P("groups"),
        P(("groups", "inst"), None),
    )
    return jax.shard_map(
        per_device,
        mesh=mesh,
        in_specs=placed,
        out_specs=(P(("groups", "inst"), None), P(("groups", "inst"), None)),
        check_vma=False,
    )
```

```python
import functools
import math

import jax
import jax.numpy as jnp
from jax import lax
from jax.experimental import pallas as pl
from jax.experimental.pallas import tpu as pltpu
from jax.sharding import PartitionSpec as P

HQ = 32
KVH = 4
HD = 128
BLK = 128
GROUP = HQ // KVH

key_rows = 512
lowest = -1e30
to_log2 = math.log2(math.e) / math.sqrt(HD)


def attend_kernel(count_ref, q_ref, k_ref, v_ref, span_k_ref, span_v_ref, out_ref, query_ref, top_ref, total_ref, acc_ref):
    rows = q_ref.shape[0]
    heads = q_ref.shape[1] // HD
    for h in range(heads):
        query_ref[h * rows : (h + 1) * rows, :] = q_ref[:, h * HD : (h + 1) * HD]

    def tile(keys, values, live, dead):
        scores = lax.dot_general(
            query_ref[...], keys, (((1,), (1,)), ((), ())), preferred_element_type=jnp.float32
        )
        parts = [scores[:, c * HD : (c + 1) * HD] for c in range(keys.shape[0] // HD)]
        if live is not None:
            parts = [jnp.where(mask, part, lowest) for mask, part in zip(live, parts)]
        top = jnp.max(functools.reduce(jnp.maximum, parts), axis=1, keepdims=True)
        if dead is None:
            top = jnp.broadcast_to(top, acc_ref.shape)
        else:
            old = top_ref[...]
            top = jnp.maximum(old, top)
            shrink = jnp.exp2((old - top) * to_log2)
        weights = [jnp.exp2((part - top) * to_log2) for part in parts]
        sums = functools.reduce(jnp.add, weights)
        rounded = jnp.concatenate([w.astype(jnp.bfloat16) for w in weights], 1)
        product = jnp.dot(rounded, values, preferred_element_type=jnp.float32)
        top_ref[...] = top
        if dead is None:
            total_ref[...] = sums
            acc_ref[...] = product
        else:
            total_ref[...] = total_ref[...] * shrink + (sums - weights[0] * dead)
            acc_ref[...] = acc_ref[...] * shrink + product

    row = lax.broadcasted_iota(jnp.int32, (rows, HD), 0)
    column = lax.broadcasted_iota(jnp.int32, (rows, HD), 1)
    causal = [
        jnp.concatenate([column + c * HD <= row] * heads, 0) for c in range(rows // HD)
    ]
    tile(span_k_ref[...], span_v_ref[...], causal, None)

    valid = count_ref[lax.axis_index("inst")] * BLK
    position = lax.broadcasted_iota(jnp.int32, (key_rows, HD), 0)
    first_lane = lax.broadcasted_iota(jnp.int32, (1, HD), 1) == 0

    def step(index, carried):
        offset = pl.multiple_of(index * key_rows, key_rows)
        keys = k_ref[pl.ds(offset, key_rows), :]
        values = v_ref[pl.ds(offset, key_rows), :]
        live = position < valid - offset
        keys = jnp.where(live, keys, jnp.broadcast_to(keys[0:1, :], keys.shape))
        values = jnp.where(live, values, jnp.zeros_like(values))
        dead = jnp.maximum(key_rows - (valid - offset), 0).astype(jnp.float32)
        tile(keys, values, None, jnp.where(first_lane, dead, 0.0))
        return carried

    lax.fori_loop(0, (valid + key_rows - 1) // key_rows, step, 0)
    mixture = acc_ref[...] / jnp.sum(total_ref[...], axis=1, keepdims=True)
    for h in range(heads):
        out_ref[:, h * HD : (h + 1) * HD] = mixture[h * rows : (h + 1) * rows].astype(jnp.bfloat16)


def attend(counts, queries, prefix_kv, span_kv, first, heads, per_step):
    rows = queries.shape[0]
    prefix_rows = prefix_kv.shape[0]
    width = per_step * HD
    start = first // per_step
    share = GROUP // per_step
    keys = rows + prefix_rows
    state = pltpu.VMEM((rows * per_step, HD), jnp.float32)
    return pl.pallas_call(
        attend_kernel,
        grid_spec=pltpu.PrefetchScalarGridSpec(
            num_scalar_prefetch=1,
            grid=(heads // per_step,),
            in_specs=[
                pl.BlockSpec((rows, width), lambda i, counts: (0, start + i)),
                pl.BlockSpec((prefix_rows, HD), lambda i, counts: (0, (start + i) // share)),
                pl.BlockSpec((prefix_rows, HD), lambda i, counts: (0, KVH + (start + i) // share)),
                pl.BlockSpec((rows, HD), lambda i, counts: (0, (start + i) // share)),
                pl.BlockSpec((rows, HD), lambda i, counts: (0, KVH + (start + i) // share)),
            ],
            out_specs=pl.BlockSpec((rows, width), lambda i, counts: (0, i)),
            scratch_shapes=[
                pltpu.VMEM((rows * per_step, HD), jnp.bfloat16),
                state,
                state,
                state,
            ],
        ),
        out_shape=jax.ShapeDtypeStruct((rows, heads * HD), jnp.bfloat16),
        compiler_params=pltpu.CompilerParams(vmem_limit_bytes=48 << 20),
        cost_estimate=pl.CostEstimate(
            flops=4 * rows * heads * HD * keys // 2,
            bytes_accessed=2 * (2 * rows * heads * HD + 2 * keys * HD * heads // per_step),
            transcendentals=rows * heads * keys // 2,
        ),
        name="attend",
    )(counts, queries, prefix_kv, prefix_kv, span_kv, span_kv)


def scatter_kernel(owner_ref, span_ref, out_ref, sems):
    rows = out_ref.shape[1]
    copies = []
    for s in range(owner_ref.shape[1]):
        page = span_ref.at[s * rows : (s + 1) * rows, :]
        copies.append(pltpu.make_async_copy(page, out_ref.at[owner_ref[0, s]], sems.at[s]))
    for copy in copies:
        copy.start()
    for copy in copies:
        copy.wait()


def scatter_pages(owners, span_kv, places):
    page_count = owners.shape[1]
    page_rows = span_kv.shape[0] // page_count
    width = span_kv.shape[1]
    return pl.pallas_call(
        scatter_kernel,
        grid_spec=pltpu.PrefetchScalarGridSpec(
            num_scalar_prefetch=1,
            grid=(),
            in_specs=[pl.BlockSpec(memory_space=pltpu.VMEM)],
            out_specs=pl.BlockSpec(memory_space=pl.ANY),
            scratch_shapes=[pltpu.SemaphoreType.DMA((page_count,))],
        ),
        out_shape=jax.ShapeDtypeStruct((places, page_rows, width), span_kv.dtype),
        name="scatter_pages",
    )(owners, span_kv)


part_plan = ((4, False), (8, True), (4, True), (8, False), (8, False))
per_step = 4


def per_device(queries, prefix_kv, span_kv, prefix_blocks, swap_flags, owners):
    inst_count = lax.axis_size("inst")
    half_count = inst_count // 2
    here = lax.axis_index("inst")

    places = jnp.arange(inst_count)
    side = (here >> 1) & 1
    lower = here - 2 * side
    mask = jnp.sum(swap_flags * ((places == lower) * 1 + (places == lower + 2) * 2))
    bases = [i for i in range(inst_count) if not i & 2]

    def far(inst):
        return (inst + half_count) % inst_count

    def send(value, hops):
        return lax.ppermute(value, "inst", hops)

    def branch(flagged):
        def run(side, counts, queries, prefix_kv, span_kv):
            if not flagged:
                return attend(counts, queries, prefix_kv, span_kv, 0, HQ, per_step)
            straight = [(i + 2 * c, far(i) + 2 * c) for c in flagged for i in bases]
            first, came, parts, pending = 0, [], [], []
            for turn, (heads, relay) in enumerate(part_plan):
                if turn == 4 and pending:
                    held = [came[at] for at in pending]
                    for at, value in zip(pending, held):
                        came[at] = send(value, over)
                part = attend(counts, queries, prefix_kv, span_kv, first, heads, per_step)
                if relay and len(flagged) == 1:
                    c = flagged[0]
                    over = [(i + 2 * (1 - c), far(i) + 2 * c) for i in bases]
                    came.append(send(part, [(i + 2 * c, i + 2 * (1 - c)) for i in bases]))
                    pending.append(turn)
                else:
                    came.append(send(part, straight))
                parts.append(part)
                first += heads
            came[:-1], parts[-1] = lax.optimization_barrier((came[:-1], parts[-1]))
            if len(flagged) == 1:
                mine = side == flagged[0]
                came = [jnp.where(mine, new, own) for new, own in zip(came, parts)]
            return jnp.concatenate(came, 1)

        return run

    outgoing = scatter_pages(owners, span_kv, inst_count)
    received = lax.all_to_all(outgoing, "inst", split_axis=0, concat_axis=0, tiled=True)
    branches = [branch([c for c in (0, 1) if m >> c & 1]) for m in range(4)]
    attended = lax.switch(mask, branches, side, prefix_blocks, queries, prefix_kv, span_kv)
    offsets = (owners[0] - here) % inst_count
    senders = (here - offsets) % inst_count
    decode_pages = received[senders].reshape(span_kv.shape)
    return (attended, decode_pages)


def solution(mesh):
    placed = (
        P(("groups", "inst"), None),
        P(("groups", "inst"), None),
        P(("groups", "inst"), None),
        P("groups"),
        P("groups"),
        P(("groups", "inst"), None),
    )
    return jax.shard_map(
        per_device,
        mesh=mesh,
        in_specs=placed,
        out_specs=(P(("groups", "inst"), None), P(("groups", "inst"), None)),
        check_vma=False,
    )
```

```python
import functools
import math

import jax
import jax.numpy as jnp
from jax import lax
from jax.experimental import pallas as pl
from jax.experimental.pallas import tpu as pltpu
from jax.sharding import PartitionSpec as P

HQ = 32
KVH = 4
HD = 128
BLK = 128
GROUP = HQ // KVH

key_rows = 512
lowest = -1e30
to_log2 = math.log2(math.e) / math.sqrt(HD)


def attend_kernel(count_ref, q_ref, k_ref, v_ref, span_k_ref, span_v_ref, out_ref, query_ref, top_ref, total_ref, acc_ref):
    rows = q_ref.shape[0]
    heads = q_ref.shape[1] // HD
    for h in range(heads):
        query_ref[h * rows : (h + 1) * rows, :] = q_ref[:, h * HD : (h + 1) * HD]

    def tile(keys, values, live, dead):
        scores = lax.dot_general(
            query_ref[...], keys, (((1,), (1,)), ((), ())), preferred_element_type=jnp.float32
        )
        parts = [scores[:, c * HD : (c + 1) * HD] for c in range(keys.shape[0] // HD)]
        if live is not None:
            parts = [jnp.where(mask, part, lowest) for mask, part in zip(live, parts)]
        top = jnp.max(functools.reduce(jnp.maximum, parts), axis=1, keepdims=True)
        if dead is None:
            top = jnp.broadcast_to(top, acc_ref.shape)
        else:
            old = top_ref[...]
            top = jnp.maximum(old, top)
            shrink = jnp.exp2((old - top) * to_log2)
        weights = [jnp.exp2((part - top) * to_log2) for part in parts]
        sums = functools.reduce(jnp.add, weights)
        rounded = jnp.concatenate([w.astype(jnp.bfloat16) for w in weights], 1)
        product = jnp.dot(rounded, values, preferred_element_type=jnp.float32)
        top_ref[...] = top
        if dead is None:
            total_ref[...] = sums
            acc_ref[...] = product
        else:
            total_ref[...] = total_ref[...] * shrink + (sums - weights[0] * dead)
            acc_ref[...] = acc_ref[...] * shrink + product

    row = lax.broadcasted_iota(jnp.int32, (rows, HD), 0)
    column = lax.broadcasted_iota(jnp.int32, (rows, HD), 1)
    causal = [
        jnp.concatenate([column + c * HD <= row] * heads, 0) for c in range(rows // HD)
    ]
    tile(span_k_ref[...], span_v_ref[...], causal, None)

    valid = count_ref[lax.axis_index("inst")] * BLK
    position = lax.broadcasted_iota(jnp.int32, (key_rows, HD), 0)
    first_lane = lax.broadcasted_iota(jnp.int32, (1, HD), 1) == 0

    def step(index, carried):
        offset = pl.multiple_of(index * key_rows, key_rows)
        keys = k_ref[pl.ds(offset, key_rows), :]
        values = v_ref[pl.ds(offset, key_rows), :]
        live = position < valid - offset
        keys = jnp.where(live, keys, jnp.broadcast_to(keys[0:1, :], keys.shape))
        values = jnp.where(live, values, jnp.zeros_like(values))
        dead = jnp.maximum(key_rows - (valid - offset), 0).astype(jnp.float32)
        tile(keys, values, None, jnp.where(first_lane, dead, 0.0))
        return carried

    lax.fori_loop(0, (valid + key_rows - 1) // key_rows, step, 0)
    mixture = acc_ref[...] / jnp.sum(total_ref[...], axis=1, keepdims=True)
    for h in range(heads):
        out_ref[:, h * HD : (h + 1) * HD] = mixture[h * rows : (h + 1) * rows].astype(jnp.bfloat16)


def attend(counts, queries, prefix_kv, span_kv, first, heads, per_step):
    rows = queries.shape[0]
    prefix_rows = prefix_kv.shape[0]
    width = per_step * HD
    start = first // per_step
    share = GROUP // per_step
    keys = rows + prefix_rows
    state = pltpu.VMEM((rows * per_step, HD), jnp.float32)
    return pl.pallas_call(
        attend_kernel,
        grid_spec=pltpu.PrefetchScalarGridSpec(
            num_scalar_prefetch=1,
            grid=(heads // per_step,),
            in_specs=[
                pl.BlockSpec((rows, width), lambda i, counts: (0, start + i)),
                pl.BlockSpec((prefix_rows, HD), lambda i, counts: (0, (start + i) // share)),
                pl.BlockSpec((prefix_rows, HD), lambda i, counts: (0, KVH + (start + i) // share)),
                pl.BlockSpec((rows, HD), lambda i, counts: (0, (start + i) // share)),
                pl.BlockSpec((rows, HD), lambda i, counts: (0, KVH + (start + i) // share)),
            ],
            out_specs=pl.BlockSpec((rows, width), lambda i, counts: (0, i)),
            scratch_shapes=[
                pltpu.VMEM((rows * per_step, HD), jnp.bfloat16),
                state,
                state,
                state,
            ],
        ),
        out_shape=jax.ShapeDtypeStruct((rows, heads * HD), jnp.bfloat16),
        compiler_params=pltpu.CompilerParams(vmem_limit_bytes=48 << 20),
        cost_estimate=pl.CostEstimate(
            flops=4 * rows * heads * HD * keys // 2,
            bytes_accessed=2 * (2 * rows * heads * HD + 2 * keys * HD * heads // per_step),
            transcendentals=rows * heads * keys // 2,
        ),
        name="attend",
    )(counts, queries, prefix_kv, prefix_kv, span_kv, span_kv)


def scatter_kernel(owner_ref, flag_ref, span_ref, out_ref, choice_ref, sems):
    rows = out_ref.shape[1]
    copies = []
    for s in range(owner_ref.shape[1]):
        page = span_ref.at[s * rows : (s + 1) * rows, :]
        copies.append(pltpu.make_async_copy(page, out_ref.at[owner_ref[0, s]], sems.at[s]))
    for copy in copies:
        copy.start()
    here = lax.axis_index("inst")
    side = (here >> 1) & 1
    own_flag = flag_ref[here]
    next_flag = flag_ref[here ^ 2]

    def weigh(at, lean):
        return lean + flag_ref[at] * (2 * ((at >> 1) & 1) - 1)

    lean = lax.fori_loop(0, flag_ref.shape[0], weigh, jnp.int32(0))
    flagged_side = jnp.where(own_flag == 1, side, 1 - side)
    heavy = lean * (2 * flagged_side - 1) > 0
    relayed = jnp.logical_and(own_flag != next_flag, heavy)
    choice_ref[0] = jnp.where(relayed, 2 + flagged_side, own_flag)
    for copy in copies:
        copy.wait()


def scatter_pages(owners, flags, span_kv, places):
    page_count = owners.shape[1]
    page_rows = span_kv.shape[0] // page_count
    width = span_kv.shape[1]
    return pl.pallas_call(
        scatter_kernel,
        grid_spec=pltpu.PrefetchScalarGridSpec(
            num_scalar_prefetch=2,
            grid=(),
            in_specs=[pl.BlockSpec(memory_space=pltpu.VMEM)],
            out_specs=[pl.BlockSpec(memory_space=pl.ANY), pl.BlockSpec(memory_space=pltpu.SMEM)],
            scratch_shapes=[pltpu.SemaphoreType.DMA((page_count,))],
        ),
        out_shape=[
            jax.ShapeDtypeStruct((places, page_rows, width), span_kv.dtype),
            jax.ShapeDtypeStruct((1,), jnp.int32),
        ],
        name="scatter_pages",
    )(owners, flags, span_kv)


part_plan = ((4, False), (8, True), (4, True), (8, False), (8, False))
per_step = 4


def per_device(queries, prefix_kv, span_kv, prefix_blocks, swap_flags, owners):
    inst_count = lax.axis_size("inst")
    half_count = inst_count // 2
    here = lax.axis_index("inst")

    side = (here >> 1) & 1
    bases = [i for i in range(inst_count) if not i & 2]

    def far(inst):
        return (inst + half_count) % inst_count

    def send(value, hops):
        return lax.ppermute(value, "inst", hops)

    def branch(flagged):
        def run(side, counts, queries, prefix_kv, span_kv):
            if not flagged:
                return attend(counts, queries, prefix_kv, span_kv, 0, HQ, per_step)
            straight = [(i + 2 * c, far(i) + 2 * c) for c in flagged for i in bases]
            first, came, parts, pending = 0, [], [], []
            for turn, (heads, relay) in enumerate(part_plan):
                if turn == 4 and pending:
                    held = [came[at] for at in pending]
                    for at, value in zip(pending, held):
                        came[at] = send(value, over)
                part = attend(counts, queries, prefix_kv, span_kv, first, heads, per_step)
                if relay and len(flagged) == 1:
                    c = flagged[0]
                    over = [(i + 2 * (1 - c), far(i) + 2 * c) for i in bases]
                    came.append(send(part, [(i + 2 * c, i + 2 * (1 - c)) for i in bases]))
                    pending.append(turn)
                else:
                    came.append(send(part, straight))
                parts.append(part)
                first += heads
            came[:-1], parts[-1] = lax.optimization_barrier((came[:-1], parts[-1]))
            if len(flagged) == 1:
                mine = side == flagged[0]
                came = [jnp.where(mine, new, own) for new, own in zip(came, parts)]
            return jnp.concatenate(came, 1)

        return run

    outgoing, choice = scatter_pages(owners, swap_flags, span_kv, inst_count)
    received = lax.all_to_all(outgoing, "inst", split_axis=0, concat_axis=0, tiled=True)
    branches = [branch([]), branch([0, 1]), branch([0]), branch([1])]
    attended = lax.switch(choice[0], branches, side, prefix_blocks, queries, prefix_kv, span_kv)
    offsets = (owners[0] - here) % inst_count
    senders = (here - offsets) % inst_count
    decode_pages = received[senders].reshape(span_kv.shape)
    return (attended, decode_pages)


def solution(mesh):
    placed = (
        P(("groups", "inst"), None),
        P(("groups", "inst"), None),
        P(("groups", "inst"), None),
        P("groups"),
        P("groups"),
        P(("groups", "inst"), None),
    )
    return jax.shard_map(
        per_device,
        mesh=mesh,
        in_specs=placed,
        out_specs=(P(("groups", "inst"), None), P(("groups", "inst"), None)),
        check_vma=False,
    )
```
